32 devices in a mesh: parts: 2 (over x), sta: 16 (over z, y, core).
Axes of the slice: x: 2, y: 2, z: 4, core: 2. Of those that a mesh axis runs over, the one named last changes fastest.
Arguments:
- raw_traces: bfloat16 [512, 16384], P('parts', 'sta'), parts along dimension 0, may hold values from -6 to 6
- filter_taps: bfloat16 [256], replicated, may hold values from -0.375 to 0.375
- station_order: int32 [512], P('parts'), parts along dimension 0, may hold values from 0 to 255, each once
- window_starts: int32 [32], P('parts'), parts along dimension 0, may hold values from 0 to 2048, as said below
- pairing: int32 [4, 16], replicated, may hold values from 0 to 15, as said below
Outputs:
- correlation: float32 [4, 512, 16, 256], P(None, ('parts', 'sta')), parts along dimension 1
The draws below stay inside these ranges and needn't reach their ends.
There are 2 independent parts, one for each index of `parts`. The reference program is written for one: setup_inputs(seed, part) draws one part's arguments, and reference() takes and returns one part's arrays. A program takes and returns all parts, laid end to end along the dimension named above; an argument that names none is the same for every part. Nothing has to cross between parts.
Inputs may be any that keep to these rules, and one draw needn't show every extreme that they name: Each station appears once; block b holds the stations station_order[b * 16 + j], j < 16. `window_starts`: starts never fall; the first is 0 and the last is 2048; consecutive starts differ by at most 273. Row r is one round of a single round-robin tournament over the 16 blocks: pairing[r, pairing[r, b]] = b, pairing[r, b] != b, and no two rows pair the same two blocks.
All inputs are finite; a program needn't handle non-finite values.
Results may differ from the reference program's by a relative error of at most 0.0049.
Values may be sent and summed in bfloat16 or wider, within the bound.
A program may use at most 128 MiB of HBM per device.

```python
import math
import jax
import jax.numpy as jnp
from jax import lax

SB = 16
NW = 16
DEC = 4
TAPS = 256
SEG = 2048
BAND = 64
LAGS = 256
ROUNDS = 4
BINS = 1024
BLOCKS = 16
STATIONS = 256
TIME = 16384
SAMPLES = 4096


def draw_window_starts(key, part):
    free_room = SAMPLES - SEG
    stride = free_room // (NW - 1)
    window_index = jnp.arange(NW, dtype=jnp.int32)
    anchor = window_index * free_room // (NW - 1)
    jitter = jax.random.randint(key, (NW,), 0, stride + 1, dtype=jnp.int32) * (window_index > 0).astype(jnp.int32)
    return jnp.minimum(anchor + jitter, free_room).astype(jnp.int32)


def draw_pairing(key, part):
    relabel = jax.random.permutation(jax.random.fold_in(key, 7), BLOCKS).astype(jnp.int32)
    inverse = jnp.argsort(relabel).astype(jnp.int32)
    rounds_col = jnp.arange(1, ROUNDS + 1, dtype=jnp.int32)[:, None]
    labels = relabel[None, :]
    mirror = (2 * rounds_col - labels) % (BLOCKS - 1)
    partner_label = jnp.where(labels == BLOCKS - 1, rounds_col % (BLOCKS - 1), jnp.where(mirror == labels, BLOCKS - 1, mirror))
    return jnp.take(inverse, partner_label).astype(jnp.int32)


def shard_levels(own_key, dims, split, least, largest):
    loudness = 1.0
    for position, parts in split:
        heights = jax.random.uniform(jax.random.fold_in(jax.random.fold_in(own_key, 6), position), (parts,), jnp.float32, least / len(split), largest / len(split))
        loudness = loudness * jnp.repeat(jnp.exp(heights), dims[position] // parts).reshape((-1,) + (1,) * (len(dims) - 1 - position))
    return loudness


def centred(stream_key, dims, width, limit, cuts=(), kind=jnp.bfloat16):
    factor_of = shard_levels(stream_key, dims, cuts, -0.22, 0.18) if cuts else 1.0
    entries = jax.random.normal(stream_key, dims, jnp.float32) * width * factor_of
    return jnp.minimum(jnp.maximum(entries, -limit), limit).astype(kind)


def setup_inputs(seed: int = 0, part: int = 0) -> dict:
    key_of = jax.random.split(jax.random.key(seed), 6)
    part_splits = jax.random.split(jax.random.fold_in(key_of[5], part), 6)
    raw_traces = centred(part_splits[0], (STATIONS, TIME), 1.0, 6.0, ((1, 16),))
    filter_taps = centred(key_of[1], (TAPS,), TAPS ** -0.5, 0.375)
    station_order = jax.random.permutation(part_splits[2], STATIONS).astype(jnp.int32)
    window_starts = draw_window_starts(jax.random.fold_in(jax.random.fold_in(key_of[5], part), 71), part)
    pairing = draw_pairing(jax.random.fold_in(key_of[5], 71), part)
    return {"raw_traces": raw_traces, "filter_taps": filter_taps, "station_order": station_order, "window_starts": window_starts, "pairing": pairing}


def decimate(signal, leading, filter_taps, factor):
    row_count, length = signal.shape
    outputs = length // factor
    per_tile = math.gcd(outputs, 128)
    tile_span = per_tile * factor
    margin = leading.shape[1]
    pieces = 1 + (margin + tile_span - 1) // tile_span
    tile_count = outputs // per_tile
    padded = jnp.concatenate([leading, signal, jnp.zeros((row_count, (pieces - 1) * tile_span - margin), signal.dtype)], axis=1)
    tap_count = filter_taps.shape[0]
    positions = jnp.arange(pieces * tile_span, dtype=jnp.int32)[:, None]
    column = jnp.arange(per_tile, dtype=jnp.int32)[None, :]
    tap_index = column * factor + tap_count - 1 - positions
    inside = (tap_index >= 0) & (tap_index < tap_count)
    banded = jnp.where(inside, jnp.take(filter_taps, jnp.clip(tap_index, 0, tap_count - 1)), jnp.zeros((), filter_taps.dtype))
    summed = jnp.zeros((row_count, tile_count, per_tile), jnp.float32)
    for section_index in range(pieces):
        segment = padded[:, section_index * tile_span:section_index * tile_span + length].reshape(row_count, tile_count, tile_span)
        summed = summed + jnp.einsum('rtu,ui->rti', segment.astype(jnp.float32), banded[section_index * tile_span:(section_index + 1) * tile_span].astype(jnp.float32), precision=lax.Precision.HIGHEST)
    return summed.reshape(row_count, outputs)

def dft_matrix(seg_length, bin_count):
    sample = jnp.arange(seg_length, dtype=jnp.int32)
    frequency = jnp.arange(bin_count, dtype=jnp.int32)
    angles = (frequency[:, None] * sample[None, :] % seg_length).astype(jnp.float32) * (2.0 * math.pi / seg_length)
    taper_curve = 0.5 - 0.5 * jnp.cos(sample.astype(jnp.float32) * (2.0 * math.pi / seg_length))
    joined = jnp.concatenate([jnp.cos(angles) * taper_curve[None, :], -jnp.sin(angles) * taper_curve[None, :]], axis=0)
    return joined.astype(jnp.bfloat16)

def lag_matrix(seg_length, bin_count, lag_count, window_count):
    frequency = jnp.arange(bin_count, dtype=jnp.int32)
    lag_offset = jnp.arange(lag_count, dtype=jnp.int32) - lag_count // 2 + seg_length
    angles = (frequency[:, None] * lag_offset[None, :] % seg_length).astype(jnp.float32) * (2.0 * math.pi / seg_length)
    normalizer = 1.0 / math.sqrt(bin_count * window_count)
    return jnp.stack([jnp.cos(angles) * normalizer, -jnp.sin(angles) * normalizer]).astype(jnp.bfloat16)

def whiten(spectrum, band_width):
    halves, bin_count, station_count, window_count = spectrum.shape
    grouped = spectrum.reshape(halves, bin_count // band_width, band_width, station_count, window_count)
    band_level = lax.optimization_barrier(jnp.sum(grouped * grouped, axis=(0, 2))) / (2 * band_width)
    scaled = grouped * (1.0 / jnp.sqrt(band_level + 1e-06))[None, :, None]
    return scaled.reshape(spectrum.shape).astype(jnp.bfloat16)

def cross_spectra(left_spec, right_spec):
    left_wide = left_spec.astype(jnp.float32)
    right_wide = right_spec.astype(jnp.float32)
    turned = jnp.stack([right_wide, jnp.stack([-right_wide[1], right_wide[0]])])
    return jnp.einsum('cfsw,kcftw->kfst', left_wide, turned, precision=lax.Precision.HIGHEST)

def reference(raw_traces, filter_taps, station_order, window_starts, pairing):
    ordered = jnp.take(raw_traces, station_order, axis=0)
    leading = jnp.zeros((STATIONS, TAPS - DEC), raw_traces.dtype)
    low_rate = lax.optimization_barrier(decimate(ordered, leading, filter_taps, DEC).astype(jnp.bfloat16))
    dft_table = lax.optimization_barrier(dft_matrix(SEG, BINS)).astype(jnp.float32)

    def block_spectra(block_rows):
        windows = jax.vmap(lambda first_sample: lax.dynamic_slice_in_dim(block_rows, first_sample, SEG, 1))(window_starts)
        spectrum = jnp.einsum('kl,wsl->ksw', dft_table, windows.astype(jnp.float32), precision=lax.Precision.HIGHEST)
        return lax.optimization_barrier(whiten(spectrum.reshape(2, BINS, SB, NW), BAND))
    whitened = lax.map(block_spectra, low_rate.reshape(BLOCKS, SB, SAMPLES))
    lag_table = lax.optimization_barrier(lag_matrix(SEG, BINS, LAGS, NW)).astype(jnp.float32)

    def one_round(partners):

        def one_block(block_index):
            own_spec = whitened[block_index]
            theirs = whitened[partners[block_index]]
            cross_spec = lax.optimization_barrier(cross_spectra(own_spec, theirs).astype(jnp.bfloat16))
            flattened = cross_spec.astype(jnp.float32).reshape(2, BINS, SB * SB)
            return jnp.einsum('kfp,kfl->pl', flattened, lag_table, precision=lax.Precision.HIGHEST).reshape(SB, SB, LAGS)
        return lax.map(one_block, jnp.arange(BLOCKS, dtype=jnp.int32)).reshape(BLOCKS * SB, SB, LAGS)
    return lax.map(one_round, pairing)
```

```python
import functools
import math

import jax
import jax.numpy as jnp
import ml_dtypes
import numpy as np
from jax import lax
from jax.experimental import pallas as pl
from jax.experimental.pallas import tpu as pltpu
from jax.sharding import PartitionSpec as P

SB = 16
DEC = 4
TAPS = 256
SEG = 2048
BAND = 64
LAGS = 256
ROUNDS = 4
BINS = 1024
LANE = 128
SPAN = LANE * DEC + TAPS
GROUPS = ROUNDS + 1
ROWS = GROUPS * SB
FT = 128
TILES = BINS // FT


def dft_tiles():
    sample = np.arange(SEG)
    frequency = np.arange(BINS)
    angles = (sample[:, None] * frequency[None, :] % SEG) * (2.0 * math.pi / SEG)
    taper = (0.5 - 0.5 * np.cos(sample * (2.0 * math.pi / SEG)))[:, None]
    both = np.stack([np.cos(angles) * taper, -np.sin(angles) * taper], axis=1)
    both = both.reshape(SEG, 2, TILES, FT).transpose(2, 0, 1, 3).reshape(TILES, SEG, 2 * FT)
    return both.astype(np.float32).astype(ml_dtypes.bfloat16)


def lag_tiles(window_count):
    frequency = np.arange(BINS)
    offset = np.arange(LAGS) - LAGS // 2 + SEG
    angles = (frequency[:, None] * offset[None, :] % SEG) * (2.0 * math.pi / SEG)
    scale = 1.0 / math.sqrt(BINS * window_count)
    both = np.stack([np.cos(angles) * scale, -np.sin(angles) * scale])
    both = both.reshape(2, TILES, FT, LAGS).transpose(1, 0, 2, 3).reshape(TILES, 2 * FT, LAGS)
    return both.astype(np.float32).astype(ml_dtypes.bfloat16)


def band_ones():
    same = np.arange(FT)[:, None] // BAND == np.arange(FT)[None, :] // BAND
    return np.concatenate([same, same]).astype(ml_dtypes.bfloat16)


def filter_kernel(raw_ref, halo_ref, taps_ref, order_ref, low_ref):
    stations = raw_ref.shape[0]
    banded = jnp.broadcast_to(taps_ref[...], (LANE, SPAN))
    banded = pltpu.roll(banded, 0, 1, stride=DEC, stride_axis=0).astype(jnp.bfloat16)
    picks = (lax.broadcasted_iota(jnp.int32, (stations, stations), 1) == order_ref[...]).astype(
        jnp.float32
    ).astype(jnp.bfloat16)
    dims = (((1,), (1,)), ((), ()))
    pieces = raw_ref.shape[1] // (LANE * DEC)
    for piece in range(pieces):
        first = piece * LANE * DEC - TAPS
        if piece == 0:
            samples = jnp.concatenate([halo_ref[...], raw_ref[:, : LANE * DEC]], axis=1)
        else:
            samples = raw_ref[:, first : first + SPAN]
        low = lax.dot_general(samples, banded, dims, preferred_element_type=jnp.float32)
        ordered = jnp.dot(picks, low.astype(jnp.bfloat16), preferred_element_type=jnp.float32)
        low_ref[piece] = ordered.astype(jnp.bfloat16)


def correlate_kernel(
    starts_ref, groups_ref, low_ref, dft_ref, lag_ref, ones_ref, out_ref, rows, windows, white, cross, sems
):
    tile = pl.program_id(0)
    planes = low_ref.shape[0]
    window_count = starts_ref.shape[0]

    @pl.when(tile == 0)
    def _():
        copies = []
        for g in range(GROUPS):
            first = pl.multiple_of(groups_ref[g] * SB, SB)
            copy = pltpu.make_async_copy(
                low_ref.at[:, pl.ds(first, SB), :],
                rows.at[pl.ds(0, planes), pl.ds(g * SB, SB), :],
                sems.at[g],
            )
            copy.start()
            copies.append(copy)
        rows[planes] = jnp.zeros((ROWS, LANE), jnp.bfloat16)
        for copy in copies:
            copy.wait()
        lane = lax.broadcasted_iota(jnp.int32, (ROWS, LANE), 1)

        def one_window(w, carry):
            start = starts_ref[w]
            plane = start // LANE
            left = LANE - start % LANE
            back = left % LANE
            now = pltpu.roll(rows[plane].astype(jnp.float32), back, 1)
            for piece in range(SEG // LANE):
                later = pltpu.roll(rows[plane + piece + 1].astype(jnp.float32), back, 1)
                windows[
                    pl.ds(pl.multiple_of(w * ROWS, SB), ROWS), piece * LANE : (piece + 1) * LANE
                ] = jnp.where(lane < left, now, later).astype(jnp.bfloat16)
                now = later
            return carry

        lax.fori_loop(0, window_count, one_window, 0)
        out_ref[...] = jnp.zeros_like(out_ref)

    per_chunk = 4

    def one_chunk(n, carry):
        chunk = windows[pl.ds(pl.multiple_of(n * per_chunk * ROWS, SB), per_chunk * ROWS), :]
        spectrum = jnp.dot(chunk, dft_ref[0], preferred_element_type=jnp.float32)
        real, imag = spectrum[:, :FT], spectrum[:, FT:]
        power = real * real + imag * imag
        high = power.astype(jnp.bfloat16)
        low = (power - high.astype(jnp.float32)).astype(jnp.bfloat16)
        level = jnp.dot(
            jnp.concatenate([high, low], axis=1), ones_ref[...], preferred_element_type=jnp.float32
        )
        scale = lax.rsqrt(level * (1.0 / (2 * BAND)) + 1e-06)
        for c, part in enumerate((real, imag)):
            rounded = (part * scale).astype(jnp.bfloat16).astype(jnp.float32)
            white[c, pl.ds(n * per_chunk, per_chunk)] = rounded.reshape(per_chunk, ROWS, FT)
        return carry

    lax.fori_loop(0, window_count // per_chunk, one_chunk, 0)

    pair = 2

    def one_pair(n, carry):
        re = [[jnp.zeros((SB, FT), jnp.float32)] * ROUNDS for _ in range(pair)]
        im = [[jnp.zeros((SB, FT), jnp.float32)] * ROUNDS for _ in range(pair)]
        for w in range(window_count):
            own = [
                [
                    jnp.broadcast_to(white[c, w, pl.ds(n * pair + p, 1), :], (SB, FT))
                    for c in range(2)
                ]
                for p in range(pair)
            ]
            for r in range(ROUNDS):
                theirs = [white[c, w, (r + 1) * SB : (r + 2) * SB, :] for c in range(2)]
                for p in range(pair):
                    re[p][r] = re[p][r] + own[p][0] * theirs[0] + own[p][1] * theirs[1]
                    im[p][r] = im[p][r] + own[p][1] * theirs[0] - own[p][0] * theirs[1]
        for p in range(pair):
            for r in range(ROUNDS):
                at = pl.ds(pl.multiple_of((n * pair + p) * SB, SB), SB)
                cross[r, at, :FT] = re[p][r].astype(jnp.bfloat16)
                cross[r, at, FT:] = im[p][r].astype(jnp.bfloat16)
        return carry

    lax.fori_loop(0, SB // pair, one_pair, 0)
    for r in range(ROUNDS):
        out_ref[r] += jnp.dot(cross[r], lag_ref[0], preferred_element_type=jnp.float32)


def body(raw_traces, filter_taps, station_order, window_starts, pairing):
    members = lax.axis_size("sta")
    me = lax.axis_index("sta")
    stations, local_time = raw_traces.shape
    window_count = window_starts.shape[0]
    pieces = local_time // (LANE * DEC)
    halo = lax.ppermute(
        raw_traces[:, local_time - TAPS :], "sta", [(i, i + 1) for i in range(members - 1)]
    )
    taps = jnp.pad(filter_taps.astype(jnp.float32)[::-1], (DEC, SPAN - TAPS - DEC)).reshape(1, SPAN)
    low = pl.pallas_call(
        filter_kernel,
        out_shape=jax.ShapeDtypeStruct((pieces, stations, LANE), jnp.bfloat16),
        compiler_params=pltpu.CompilerParams(vmem_limit_bytes=40 * 2**20),
    )(raw_traces, halo, taps, station_order.reshape(stations, 1))
    low = lax.all_gather(low, "sta", axis=0, tiled=True)
    groups = jnp.concatenate([me[None].astype(jnp.int32), lax.dynamic_slice_in_dim(pairing, me, 1, 1)[:, 0]])
    planes = low.shape[0]
    grid_spec = pltpu.PrefetchScalarGridSpec(
        num_scalar_prefetch=2,
        grid=(TILES,),
        in_specs=[
            pl.BlockSpec(memory_space=pl.ANY),
            pl.BlockSpec((1, SEG, 2 * FT), lambda n, *_: (n, 0, 0)),
            pl.BlockSpec((1, 2 * FT, LAGS), lambda n, *_: (n, 0, 0)),
            pl.BlockSpec((2 * FT, FT), lambda n, *_: (0, 0)),
        ],
        out_specs=pl.BlockSpec((ROUNDS, SB * SB, LAGS), lambda n, *_: (0, 0, 0)),
        scratch_shapes=[
            pltpu.VMEM((planes + 1, ROWS, LANE), jnp.bfloat16),
            pltpu.VMEM((window_count * ROWS, SEG), jnp.bfloat16),
            pltpu.VMEM((2, window_count, ROWS, FT), jnp.float32),
            pltpu.VMEM((ROUNDS, SB * SB, 2 * FT), jnp.bfloat16),
            pltpu.SemaphoreType.DMA((GROUPS,)),
        ],
    )
    correlated = pl.pallas_call(
        correlate_kernel,
        grid_spec=grid_spec,
        out_shape=jax.ShapeDtypeStruct((ROUNDS, SB * SB, LAGS), jnp.float32),
        compiler_params=pltpu.CompilerParams(vmem_limit_bytes=48 * 2**20),
    )(
        window_starts,
        groups,
        low,
        jnp.asarray(dft_tiles()),
        jnp.asarray(lag_tiles(window_count)),
        jnp.asarray(band_ones()),
    )
    return correlated.reshape(ROUNDS, SB, SB, LAGS)


def solution(mesh):
    return jax.shard_map(
        body,
        mesh=mesh,
        in_specs=(P("parts", "sta"), P(), P("parts"), P("parts"), P()),
        out_specs=P(None, ("parts", "sta"), None, None),
        check_vma=False,
    )
```

```python
import functools
import math

import jax
import jax.numpy as jnp
import ml_dtypes
import numpy as np
from jax import lax
from jax.experimental import pallas as pl
from jax.experimental.pallas import tpu as pltpu
from jax.sharding import PartitionSpec as P

SB = 16
DEC = 4
TAPS = 256
SEG = 2048
BAND = 64
LAGS = 256
ROUNDS = 4
BINS = 1024
LANE = 128
SPAN = LANE * DEC + TAPS
GROUPS = ROUNDS + 1
ROWS = GROUPS * SB
FT = 128
TILES = BINS // FT
QUAD = 4
MESH = pl.DeviceIdType.MESH


def dft_tiles():
    sample = np.arange(SEG)
    frequency = np.arange(BINS)
    angles = (sample[:, None] * frequency[None, :] % SEG) * (2.0 * math.pi / SEG)
    taper = (0.5 - 0.5 * np.cos(sample * (2.0 * math.pi / SEG)))[:, None]
    both = np.stack([np.cos(angles) * taper, -np.sin(angles) * taper], axis=1)
    both = both.reshape(SEG, 2, TILES, FT).transpose(2, 0, 1, 3).reshape(TILES, SEG, 2 * FT)
    return both.astype(np.float32).astype(ml_dtypes.bfloat16)


def lag_tiles(window_count):
    frequency = np.arange(BINS)
    offset = np.arange(LAGS) - LAGS // 2 + SEG
    angles = (frequency[:, None] * offset[None, :] % SEG) * (2.0 * math.pi / SEG)
    scale = 1.0 / math.sqrt(BINS * window_count)
    both = np.stack([np.cos(angles) * scale, -np.sin(angles) * scale])
    both = both.reshape(2, TILES, FT, LAGS).transpose(1, 0, 2, 3).reshape(TILES, 2 * FT, LAGS)
    return both.astype(np.float32).astype(ml_dtypes.bfloat16)


def band_ones():
    same = np.arange(FT)[:, None] // BAND == np.arange(FT)[None, :] // BAND
    return np.concatenate([same, same]).astype(ml_dtypes.bfloat16)


def gather_kernel(members, raw_ref, taps_ref, order_ref, out_ref, halo, low, halo_sems, own_sem, send_sems, recv_sems):
    me = lax.axis_index("sta")
    stations, local_time = raw_ref.shape
    line = members // QUAD
    rank, lead = me // QUAD, me % QUAD
    far = [lax.rem(rank + k, line) * QUAD + lead for k in range(1, line)]
    across = rank * QUAD + lax.rem(lead + 2, QUAD)
    twin = me + 1 - 2 * lax.rem(me, 2)
    after, before = lax.rem(me + 1, members), lax.rem(me + members - 1, members)

    barrier = pltpu.get_barrier_semaphore()
    greeted = far + [across, twin, after, before]
    for peer in greeted:
        pl.semaphore_signal(barrier, inc=1, device_id={"sta": peer}, device_id_type=MESH)
    pl.semaphore_wait(barrier, len(greeted))

    halo_copy = pltpu.make_async_remote_copy(
        src_ref=raw_ref.at[:, local_time - TAPS :],
        dst_ref=halo,
        send_sem=halo_sems.at[0],
        recv_sem=halo_sems.at[1],
        device_id={"sta": after},
        device_id_type=MESH,
    )

    @pl.when(me < members - 1)
    def _():
        halo_copy.start()

    banded = jnp.broadcast_to(taps_ref[...], (LANE, SPAN))
    banded = pltpu.roll(banded, 0, 1, stride=DEC, stride_axis=0).astype(jnp.bfloat16)
    picks = (lax.broadcasted_iota(jnp.int32, (stations, stations), 1) == order_ref[...]).astype(
        jnp.float32
    ).astype(jnp.bfloat16)
    dims = (((1,), (1,)), ((), ()))

    def filtered(piece, samples):
        summed = lax.dot_general(samples, banded, dims, preferred_element_type=jnp.float32)
        ordered = jnp.dot(picks, summed.astype(jnp.bfloat16), preferred_element_type=jnp.float32)
        low[piece] = ordered.astype(jnp.bfloat16)

    for piece in range(1, low.shape[0]):
        first = piece * LANE * DEC - TAPS
        filtered(piece, raw_ref[:, first : first + SPAN])

    @pl.when(me > 0)
    def _():
        halo_copy.wait_recv()

    @pl.when(me == 0)
    def _():
        halo[...] = jnp.zeros_like(halo)

    filtered(0, jnp.concatenate([halo[...], raw_ref[:, : LANE * DEC]], axis=1))

    sent = []

    def send(source, slot, peer):
        n = len(sent)
        copy = pltpu.make_async_remote_copy(
            src_ref=source,
            dst_ref=out_ref.at[slot],
            send_sem=send_sems.at[n],
            recv_sem=recv_sems.at[slot],
            device_id={"sta": peer},
            device_id_type=MESH,
        )
        copy.start()
        sent.append(copy)

    def arrived(slot):
        pltpu.make_async_remote_copy(
            src_ref=low,
            dst_ref=out_ref.at[slot],
            send_sem=send_sems.at[0],
            recv_sem=recv_sems.at[slot],
            device_id={"sta": twin},
            device_id_type=MESH,
        ).wait_recv()

    order = sorted(range(line - 1), key=lambda k: min(k + 1, line - 1 - k))
    for k in order:
        send(low, me, far[k])
    send(low, me, across)
    send(low, me, twin)
    own = pltpu.make_async_copy(low, out_ref.at[me], own_sem)
    own.start()
    shift = across - me
    arrived(me + shift)
    send(out_ref.at[me + shift], me + shift, twin)
    for k in order:
        arrived(far[k])
        send(out_ref.at[far[k]], far[k], across)
        send(out_ref.at[far[k]], far[k], twin)
    for k in order:
        arrived(far[k] + shift)
        send(out_ref.at[far[k] + shift], far[k] + shift, twin)
    turn = twin - me
    for slot in [me] + [far[k] for k in order]:
        arrived(slot + turn)
        arrived(slot + shift + turn)
    own.wait()
    for copy in sent:
        copy.wait_send()

    @pl.when(me < members - 1)
    def _():
        halo_copy.wait_send()


def correlate_kernel(
    starts_ref, groups_ref, low_ref, dft_ref, lag_ref, ones_ref, out_ref, rows, windows, white, cross, sems
):
    tile = pl.program_id(0)
    planes = low_ref.shape[0]
    window_count = starts_ref.shape[0]

    @pl.when(tile == 0)
    def _():
        copies = []
        for g in range(GROUPS):
            first = pl.multiple_of(groups_ref[g] * SB, SB)
            copy = pltpu.make_async_copy(
                low_ref.at[:, pl.ds(first, SB), :],
                rows.at[pl.ds(0, planes), pl.ds(g * SB, SB), :],
                sems.at[g],
            )
            copy.start()
            copies.append(copy)
        rows[planes] = jnp.zeros((ROWS, LANE), jnp.bfloat16)
        for copy in copies:
            copy.wait()
        lane = lax.broadcasted_iota(jnp.int32, (ROWS, LANE), 1)

        def one_window(w, carry):
            start = starts_ref[w]
            plane = start // LANE
            left = LANE - start % LANE
            back = left % LANE
            now = pltpu.roll(rows[plane].astype(jnp.float32), back, 1)
            for piece in range(SEG // LANE):
                later = pltpu.roll(rows[plane + piece + 1].astype(jnp.float32), back, 1)
                windows[
                    pl.ds(pl.multiple_of(w * ROWS, SB), ROWS), piece * LANE : (piece + 1) * LANE
                ] = jnp.where(lane < left, now, later).astype(jnp.bfloat16)
                now = later
            return carry

        lax.fori_loop(0, window_count, one_window, 0)
        out_ref[...] = jnp.zeros_like(out_ref)

    per_chunk = 4

    def one_chunk(n, carry):
        chunk = windows[pl.ds(pl.multiple_of(n * per_chunk * ROWS, SB), per_chunk * ROWS), :]
        spectrum = jnp.dot(chunk, dft_ref[0], preferred_element_type=jnp.float32)
        real, imag = spectrum[:, :FT], spectrum[:, FT:]
        power = real * real + imag * imag
        high = power.astype(jnp.bfloat16)
        low = (power - high.astype(jnp.float32)).astype(jnp.bfloat16)
        level = jnp.dot(
            jnp.concatenate([high, low], axis=1), ones_ref[...], preferred_element_type=jnp.float32
        )
        scale = lax.rsqrt(level * (1.0 / (2 * BAND)) + 1e-06)
        for c, part in enumerate((real, imag)):
            rounded = (part * scale).astype(jnp.bfloat16).astype(jnp.float32)
            white[c, pl.ds(n * per_chunk, per_chunk)] = rounded.reshape(per_chunk, ROWS, FT)
        return carry

    lax.fori_loop(0, window_count // per_chunk, one_chunk, 0)

    pair = 2

    def one_pair(n, carry):
        re = [[jnp.zeros((SB, FT), jnp.float32)] * ROUNDS for _ in range(pair)]
        im = [[jnp.zeros((SB, FT), jnp.float32)] * ROUNDS for _ in range(pair)]
        for w in range(window_count):
            own = [
                [
                    jnp.broadcast_to(white[c, w, pl.ds(n * pair + p, 1), :], (SB, FT))
                    for c in range(2)
                ]
                for p in range(pair)
            ]
            for r in range(ROUNDS):
                theirs = [white[c, w, (r + 1) * SB : (r + 2) * SB, :] for c in range(2)]
                for p in range(pair):
                    re[p][r] = re[p][r] + own[p][0] * theirs[0] + own[p][1] * theirs[1]
                    im[p][r] = im[p][r] + own[p][1] * theirs[0] - own[p][0] * theirs[1]
        for p in range(pair):
            for r in range(ROUNDS):
                at = pl.ds(pl.multiple_of((n * pair + p) * SB, SB), SB)
                cross[r, at, :FT] = re[p][r].astype(jnp.bfloat16)
                cross[r, at, FT:] = im[p][r].astype(jnp.bfloat16)
        return carry

    lax.fori_loop(0, SB // pair, one_pair, 0)
    for r in range(ROUNDS):
        out_ref[r] += jnp.dot(cross[r], lag_ref[0], preferred_element_type=jnp.float32)


def body(raw_traces, filter_taps, station_order, window_starts, pairing):
    members = lax.axis_size("sta")
    me = lax.axis_index("sta")
    stations, local_time = raw_traces.shape
    window_count = window_starts.shape[0]
    pieces = local_time // (LANE * DEC)
    taps = jnp.pad(filter_taps.astype(jnp.float32)[::-1], (DEC, SPAN - TAPS - DEC)).reshape(1, SPAN)
    in_vmem = pl.BlockSpec(memory_space=pltpu.VMEM)
    low = pl.pallas_call(
        functools.partial(gather_kernel, members),
        out_shape=jax.ShapeDtypeStruct((members, pieces, stations, LANE), jnp.bfloat16),
        in_specs=[in_vmem] * 3,
        out_specs=pl.BlockSpec(memory_space=pl.ANY),
        scratch_shapes=[
            pltpu.VMEM((stations, TAPS), jnp.bfloat16),
            pltpu.VMEM((pieces, stations, LANE), jnp.bfloat16),
            pltpu.SemaphoreType.DMA((2,)),
            pltpu.SemaphoreType.DMA,
            pltpu.SemaphoreType.DMA((members,)),
            pltpu.SemaphoreType.DMA((members,)),
        ],
        compiler_params=pltpu.CompilerParams(
            collective_id=0, has_side_effects=True, vmem_limit_bytes=40 * 2**20
        ),
    )(raw_traces, taps, station_order.reshape(stations, 1))
    low = low.reshape(members * pieces, stations, LANE)
    groups = jnp.concatenate([me[None].astype(jnp.int32), lax.dynamic_slice_in_dim(pairing, me, 1, 1)[:, 0]])
    planes = low.shape[0]
    grid_spec = pltpu.PrefetchScalarGridSpec(
        num_scalar_prefetch=2,
        grid=(TILES,),
        in_specs=[
            pl.BlockSpec(memory_space=pl.ANY),
            pl.BlockSpec((1, SEG, 2 * FT), lambda n, *_: (n, 0, 0)),
            pl.BlockSpec((1, 2 * FT, LAGS), lambda n, *_: (n, 0, 0)),
            pl.BlockSpec((2 * FT, FT), lambda n, *_: (0, 0)),
        ],
        out_specs=pl.BlockSpec((ROUNDS, SB * SB, LAGS), lambda n, *_: (0, 0, 0)),
        scratch_shapes=[
            pltpu.VMEM((planes + 1, ROWS, LANE), jnp.bfloat16),
            pltpu.VMEM((window_count * ROWS, SEG), jnp.bfloat16),
            pltpu.VMEM((2, window_count, ROWS, FT), jnp.float32),
            pltpu.VMEM((ROUNDS, SB * SB, 2 * FT), jnp.bfloat16),
            pltpu.SemaphoreType.DMA((GROUPS,)),
        ],
    )
    correlated = pl.pallas_call(
        correlate_kernel,
        grid_spec=grid_spec,
        out_shape=jax.ShapeDtypeStruct((ROUNDS, SB * SB, LAGS), jnp.float32),
        compiler_params=pltpu.CompilerParams(vmem_limit_bytes=48 * 2**20),
    )(
        window_starts,
        groups,
        low,
        jnp.asarray(dft_tiles()),
        jnp.asarray(lag_tiles(window_count)),
        jnp.asarray(band_ones()),
    )
    return correlated.reshape(ROUNDS, SB, SB, LAGS)


def solution(mesh):
    return jax.shard_map(
        body,
        mesh=mesh,
        in_specs=(P("parts", "sta"), P(), P("parts"), P("parts"), P()),
        out_specs=P(None, ("parts", "sta"), None, None),
        check_vma=False,
    )
```

```python
import functools
import math

import jax
import jax.numpy as jnp
import ml_dtypes
import numpy as np
from jax import lax
from jax.experimental import pallas as pl
from jax.experimental.pallas import tpu as pltpu
from jax.sharding import PartitionSpec as P

SB = 16
DEC = 4
TAPS = 256
SEG = 2048
BAND = 64
LAGS = 256
ROUNDS = 4
BINS = 1024
LANE = 128
SPAN = LANE * DEC + TAPS
GROUPS = ROUNDS + 1
ROWS = GROUPS * SB
FT = 128
TILES = BINS // FT
QUAD = 4
MESH = pl.DeviceIdType.MESH


def dft_tiles():
    sample = np.arange(SEG)
    frequency = np.arange(BINS)
    angles = (sample[:, None] * frequency[None, :] % SEG) * (2.0 * math.pi / SEG)
    taper = (0.5 - 0.5 * np.cos(sample * (2.0 * math.pi / SEG)))[:, None]
    both = np.stack([np.cos(angles) * taper, -np.sin(angles) * taper], axis=1)
    both = both.reshape(SEG, 2, TILES, FT).transpose(2, 0, 1, 3).reshape(TILES, SEG, 2 * FT)
    return both.astype(np.float32).astype(ml_dtypes.bfloat16)


def lag_tiles(window_count):
    frequency = np.arange(BINS)
    offset = np.arange(LAGS) - LAGS // 2 + SEG
    angles = (frequency[:, None] * offset[None, :] % SEG) * (2.0 * math.pi / SEG)
    scale = 1.0 / math.sqrt(BINS * window_count)
    both = np.stack([np.cos(angles) * scale, -np.sin(angles) * scale])
    both = both.reshape(2, TILES, FT, LAGS).transpose(1, 0, 2, 3).reshape(TILES, 2 * FT, LAGS)
    return both.astype(np.float32).astype(ml_dtypes.bfloat16)


def band_ones():
    same = np.arange(FT)[:, None] // BAND == np.arange(FT)[None, :] // BAND
    return np.concatenate([same, same]).astype(ml_dtypes.bfloat16)


def gather_kernel(members, raw_ref, taps_ref, order_ref, out_ref, halo, low, halo_sems, own_sem, send_sems, recv_sems):
    me = lax.axis_index("sta")
    stations, local_time = raw_ref.shape
    line = members // QUAD
    rank, lead = me // QUAD, me % QUAD
    far = [lax.rem(rank + k, line) * QUAD + lead for k in range(1, line)]
    across = rank * QUAD + lax.rem(lead + 2, QUAD)
    twin = me + 1 - 2 * lax.rem(me, 2)
    after, before = lax.rem(me + 1, members), lax.rem(me + members - 1, members)

    barrier = pltpu.get_barrier_semaphore()
    greeted = far + [across, twin, after, before]
    for peer in greeted:
        pl.semaphore_signal(barrier, inc=1, device_id={"sta": peer}, device_id_type=MESH)
    pl.semaphore_wait(barrier, len(greeted))

    halo_copy = pltpu.make_async_remote_copy(
        src_ref=raw_ref.at[:, local_time - TAPS :],
        dst_ref=halo,
        send_sem=halo_sems.at[0],
        recv_sem=halo_sems.at[1],
        device_id={"sta": after},
        device_id_type=MESH,
    )

    @pl.when(me < members - 1)
    def _():
        halo_copy.start()

    banded = jnp.broadcast_to(taps_ref[...], (LANE, SPAN))
    banded = pltpu.roll(banded, 0, 1, stride=DEC, stride_axis=0).astype(jnp.bfloat16)
    picks = (lax.broadcasted_iota(jnp.int32, (stations, stations), 1) == order_ref[...]).astype(
        jnp.float32
    ).astype(jnp.bfloat16)
    dims = (((1,), (1,)), ((), ()))

    def filtered(piece, samples):
        summed = lax.dot_general(samples, banded, dims, preferred_element_type=jnp.float32)
        ordered = jnp.dot(picks, summed.astype(jnp.bfloat16), preferred_element_type=jnp.float32)
        low[piece] = ordered.astype(jnp.bfloat16)

    for piece in range(1, low.shape[0]):
        first = piece * LANE * DEC - TAPS
        filtered(piece, raw_ref[:, first : first + SPAN])

    @pl.when(me > 0)
    def _():
        halo_copy.wait_recv()

    @pl.when(me == 0)
    def _():
        halo[...] = jnp.zeros_like(halo)

    filtered(0, jnp.concatenate([halo[...], raw_ref[:, : LANE * DEC]], axis=1))

    sent = []

    def send(source, slot, peer):
        n = len(sent)
        copy = pltpu.make_async_remote_copy(
            src_ref=source,
            dst_ref=out_ref.at[slot],
            send_sem=send_sems.at[n],
            recv_sem=recv_sems.at[slot],
            device_id={"sta": peer},
            device_id_type=MESH,
        )
        copy.start()
        sent.append(copy)

    def arrived(slot):
        pltpu.make_async_remote_copy(
            src_ref=low,
            dst_ref=out_ref.at[slot],
            send_sem=send_sems.at[0],
            recv_sem=recv_sems.at[slot],
            device_id={"sta": twin},
            device_id_type=MESH,
        ).wait_recv()

    order = sorted(range(line - 1), key=lambda k: min(k + 1, line - 1 - k))
    for k in order:
        send(low, me, far[k])
    send(low, me, across)
    send(low, me, twin)
    own = pltpu.make_async_copy(low, out_ref.at[me], own_sem)
    own.start()
    shift = across - me
    arrived(me + shift)
    send(out_ref.at[me + shift], me + shift, twin)
    for k in order:
        arrived(far[k])
        send(out_ref.at[far[k]], far[k], across)
        send(out_ref.at[far[k]], far[k], twin)
    for k in order:
        arrived(far[k] + shift)
        send(out_ref.at[far[k] + shift], far[k] + shift, twin)
    turn = twin - me
    for slot in [me] + [far[k] for k in order]:
        arrived(slot + turn)
        arrived(slot + shift + turn)
    own.wait()
    for copy in sent:
        copy.wait_send()

    @pl.when(me < members - 1)
    def _():
        halo_copy.wait_send()


def correlate_kernel(
    starts_ref, groups_ref, low_ref, dft_ref, lag_ref, ones_ref, out_ref, rows, windows, white, cross, sems
):
    tile = pl.program_id(0)
    planes = low_ref.shape[0]
    window_count = starts_ref.shape[0]

    @pl.when(tile == 0)
    def _():
        copies = []
        for g in range(GROUPS):
            first = pl.multiple_of(groups_ref[g] * SB, SB)
            copy = pltpu.make_async_copy(
                low_ref.at[:, pl.ds(first, SB), :],
                rows.at[pl.ds(0, planes), pl.ds(g * SB, SB), :],
                sems.at[g],
            )
            copy.start()
            copies.append(copy)
        rows[planes] = jnp.zeros((ROWS, LANE), jnp.bfloat16)
        for copy in copies:
            copy.wait()
        lane = lax.broadcasted_iota(jnp.int32, (ROWS, LANE), 1)

        def one_window(w, carry):
            start = starts_ref[w]
            plane = start // LANE
            left = LANE - start % LANE
            back = left % LANE
            now = pltpu.roll(rows[plane].astype(jnp.float32), back, 1)
            for piece in range(SEG // LANE):
                later = pltpu.roll(rows[plane + piece + 1].astype(jnp.float32), back, 1)
                windows[
                    pl.ds(pl.multiple_of(w * ROWS, SB), ROWS), piece * LANE : (piece + 1) * LANE
                ] = jnp.where(lane < left, now, later).astype(jnp.bfloat16)
                now = later
            return carry

        lax.fori_loop(0, window_count, one_window, 0)
        out_ref[...] = jnp.zeros_like(out_ref)

    per_chunk = 8

    def one_chunk(n, carry):
        chunk = windows[pl.ds(pl.multiple_of(n * per_chunk * ROWS, SB), per_chunk * ROWS), :]
        spectrum = jnp.dot(chunk, dft_ref[0], preferred_element_type=jnp.float32)
        real, imag = spectrum[:, :FT], spectrum[:, FT:]
        power = real * real + imag * imag
        high = power.astype(jnp.bfloat16)
        low = (power - high.astype(jnp.float32)).astype(jnp.bfloat16)
        level = jnp.dot(
            jnp.concatenate([high, low], axis=1), ones_ref[...], preferred_element_type=jnp.float32
        )
        scale = lax.rsqrt(level * (1.0 / (2 * BAND)) + 1e-06)
        for c, part in enumerate((real, imag)):
            rounded = (part * scale).astype(jnp.bfloat16).astype(jnp.float32)
            white[c, pl.ds(n * per_chunk, per_chunk)] = rounded.reshape(per_chunk, ROWS, FT)
        return carry

    lax.fori_loop(0, window_count // per_chunk, one_chunk, 0)

    pair = 2

    def one_pair(n, carry):
        re = [[jnp.zeros((SB, FT), jnp.float32)] * ROUNDS for _ in range(pair)]
        im = [[jnp.zeros((SB, FT), jnp.float32)] * ROUNDS for _ in range(pair)]
        for w in range(window_count):
            own = [
                [
                    jnp.broadcast_to(white[c, w, pl.ds(n * pair + p, 1), :], (SB, FT))
                    for c in range(2)
                ]
                for p in range(pair)
            ]
            for r in range(ROUNDS):
                theirs = [white[c, w, (r + 1) * SB : (r + 2) * SB, :] for c in range(2)]
                for p in range(pair):
                    re[p][r] = re[p][r] + own[p][0] * theirs[0] + own[p][1] * theirs[1]
                    im[p][r] = im[p][r] + own[p][1] * theirs[0] - own[p][0] * theirs[1]
        for p in range(pair):
            for r in range(ROUNDS):
                at = pl.ds(pl.multiple_of((n * pair + p) * SB, SB), SB)
                cross[r, at, :FT] = re[p][r].astype(jnp.bfloat16)
                cross[r, at, FT:] = im[p][r].astype(jnp.bfloat16)
        return carry

    lax.fori_loop(0, SB // pair, one_pair, 0)
    for r in range(ROUNDS):
        out_ref[r] += jnp.dot(cross[r], lag_ref[0], preferred_element_type=jnp.float32)


def correlate(window_starts, groups, low, dft, lag, ones):
    window_count = window_starts.shape[0]
    planes = low.shape[0]
    grid_spec = pltpu.PrefetchScalarGridSpec(
        num_scalar_prefetch=2,
        grid=(TILES,),
        in_specs=[
            pl.BlockSpec(memory_space=pl.ANY),
            pl.BlockSpec((1, SEG, 2 * FT), lambda n, *_: (n, 0, 0)),
            pl.BlockSpec((1, 2 * FT, LAGS), lambda n, *_: (n, 0, 0)),
            pl.BlockSpec((2 * FT, FT), lambda n, *_: (0, 0)),
        ],
        out_specs=pl.BlockSpec((ROUNDS, SB * SB, LAGS), lambda n, *_: (0, 0, 0)),
        scratch_shapes=[
            pltpu.VMEM((planes + 1, ROWS, LANE), jnp.bfloat16),
            pltpu.VMEM((window_count * ROWS, SEG), jnp.bfloat16),
            pltpu.VMEM((2, window_count, ROWS, FT), jnp.float32),
            pltpu.VMEM((ROUNDS, SB * SB, 2 * FT), jnp.bfloat16),
            pltpu.SemaphoreType.DMA((GROUPS,)),
        ],
    )
    return pl.pallas_call(
        correlate_kernel,
        grid_spec=grid_spec,
        out_shape=jax.ShapeDtypeStruct((ROUNDS, SB * SB, LAGS), jnp.float32),
        compiler_params=pltpu.CompilerParams(vmem_limit_bytes=48 * 2**20),
    )(window_starts, groups, low, dft, lag, ones)


def body(raw_traces, filter_taps, station_order, window_starts, pairing):
    members = lax.axis_size("sta")
    me = lax.axis_index("sta")
    stations, local_time = raw_traces.shape
    window_count = window_starts.shape[0]
    pieces = local_time // (LANE * DEC)
    taps = jnp.pad(filter_taps.astype(jnp.float32)[::-1], (DEC, SPAN - TAPS - DEC)).reshape(1, SPAN)
    in_vmem = pl.BlockSpec(memory_space=pltpu.VMEM)
    low = pl.pallas_call(
        functools.partial(gather_kernel, members),
        out_shape=jax.ShapeDtypeStruct((members, pieces, stations, LANE), jnp.bfloat16),
        in_specs=[in_vmem] * 3,
        out_specs=pl.BlockSpec(memory_space=pl.ANY),
        scratch_shapes=[
            pltpu.VMEM((stations, TAPS), jnp.bfloat16),
            pltpu.VMEM((pieces, stations, LANE), jnp.bfloat16),
            pltpu.SemaphoreType.DMA((2,)),
            pltpu.SemaphoreType.DMA,
            pltpu.SemaphoreType.DMA((members,)),
            pltpu.SemaphoreType.DMA((members,)),
        ],
        compiler_params=pltpu.CompilerParams(
            collective_id=0, has_side_effects=True, vmem_limit_bytes=40 * 2**20
        ),
    )(raw_traces, taps, station_order.reshape(stations, 1))
    low = low.reshape(members * pieces, stations, LANE)
    groups = jnp.concatenate([me[None].astype(jnp.int32), lax.dynamic_slice_in_dim(pairing, me, 1, 1)[:, 0]])
    correlated = correlate(
        window_starts,
        groups,
        low,
        jnp.asarray(dft_tiles()),
        jnp.asarray(lag_tiles(window_count)),
        jnp.asarray(band_ones()),
    )
    return correlated.reshape(ROUNDS, SB, SB, LAGS)


def solution(mesh):
    return jax.shard_map(
        body,
        mesh=mesh,
        in_specs=(P("parts", "sta"), P(), P("parts"), P("parts"), P()),
        out_specs=P(None, ("parts", "sta"), None, None),
        check_vma=False,
    )
```
